32 devices in a mesh: groups: 2 (over y), grid: 4 (over z), feat: 4 (over x, core).
Axes of the slice: x: 2, y: 2, z: 4, core: 2. Of those that a mesh axis runs over, the one named last changes fastest.
Arguments:
- grid_state: bfloat16 [8192, 227], P(('groups', 'grid')), parts along dimension 0, may hold values from -6 to 6
- mesh_state: bfloat16 [2048, 512], P('grid', 'feat'), may hold values from -6 to 6
- enc_rows: int32 [4, 4, 32], P('grid'), may hold values from 0 to 1023
- enc_targets: int32 [4, 4, 32], P('grid'), may hold values from 0 to 512, as said below
- mesh_senders: int32 [16384], P('grid'), may hold values from 0 to 639
- mesh_receivers: int32 [16384], P('grid'), may hold values from 0 to 511
- dec_rows: int32 [4, 4, 64], P('grid'), may hold values from 0 to 511
- dec_targets: int32 [4, 4, 64], P('grid'), may hold values from 0 to 1024, as said below
- enc_grid_w: bfloat16 [227, 512], P(None, 'feat'), may hold values from -0.375 to 0.375
- enc_mesh_w: bfloat16 [512, 512], P(None, 'feat'), may hold values from -0.25 to 0.25
- enc_bias: float32 [512], P('feat'), may hold values from -3 to 3
- enc_out_w: bfloat16 [512, 512], P('feat'), may hold values from -0.25 to 0.25
- enc_gain: float32 [512], P('feat'), may hold values from 0.1 to 1.9
- proc_send_w: bfloat16 [2, 512, 512], P(None, None, 'feat'), may hold values from -0.25 to 0.25
- proc_recv_w: bfloat16 [2, 512, 512], P(None, None, 'feat'), may hold values from -0.25 to 0.25
- proc_bias: float32 [2, 512], P(None, 'feat'), may hold values from -3 to 3
- proc_out_w: bfloat16 [2, 512, 512], P(None, 'feat'), may hold values from -0.25 to 0.25
- proc_gain: float32 [2, 512], P(None, 'feat'), may hold values from 0.1 to 1.9
- dec_mesh_w: bfloat16 [512, 512], P(None, 'feat'), may hold values from -0.25 to 0.25
- dec_grid_w: bfloat16 [227, 512], P(None, 'feat'), may hold values from -0.375 to 0.375
- dec_bias: float32 [512], P('feat'), may hold values from -3 to 3
- dec_out_w: bfloat16 [512, 227], P('feat'), may hold values from -0.25 to 0.25
Outputs:
- next_state: float32 [8192, 227], P(('groups', 'grid', 'feat')), parts along dimension 0
The draws below stay inside these ranges and needn't reach their ends.
There are 2 independent parts, one for each index of `groups`. The reference program is written for one: setup_inputs(seed, part) draws one part's arguments, and reference() takes and returns one part's arrays. A program takes and returns all parts, laid end to end along the dimension named above; an argument that names none is the same for every part. Nothing has to cross between parts.
Inputs may be any that keep to these rules, and one draw needn't show every extreme that they name: `enc_targets`: value 512 marks an empty slot; in each partition pair the filled slots come first; one mesh partition has all 32 slots filled from every grid partition. `dec_targets`: value 1024 marks an empty slot; in each partition pair the filled slots come first; one grid partition has all 64 slots filled from every mesh partition.
All inputs are finite; a program needn't handle non-finite values.
Results may differ from the reference program's by a relative error of at most 0.009.
Values may be sent and summed in bfloat16 or wider, within the bound.
A program may use at most 64 MiB of HBM per device.

```python
import jax
import jax.numpy as jnp
from jax import lax

D = 512
VARS = 227
GRID_DEV = 1024
MESH_DEV = 512
HALO = 64
PROC_LAYERS = 2
CAP = 32
CAP2 = 64
EDGE_DEV = 4096
GRID_NODES = 4096
MESH_NODES = 2048
MESH_EDGES = 16384
N_GRID = 4


def fill_slots(key, owners, width, capacity):
    count_key, busy_key, value_key = jax.random.split(key, 3)
    counts = jax.random.randint(count_key, (owners, owners), capacity // 2, capacity + 1)
    busiest = jax.random.randint(busy_key, (), 0, owners)
    counts = jnp.where(jnp.arange(owners)[None, :] == busiest, capacity, counts)
    values = jax.random.randint(value_key, (owners, owners, capacity), 0, width)
    position = jnp.arange(capacity)
    return jnp.where(position[None, None, :] < counts[:, :, None], values, width).astype(jnp.int32)


def draw_enc_targets(key, part):
    key = jax.random.fold_in(key, 11)
    return fill_slots(key, N_GRID, MESH_DEV, CAP)


def draw_dec_targets(key, part):
    key = jax.random.fold_in(key, 23)
    return fill_slots(key, N_GRID, GRID_DEV, CAP2)


def place_ends(array, rng, least, top_value):
    spot = [jax.random.randint(jax.random.fold_in(rng, axis), (), 0, length) for axis, length in enumerate(array.shape)]
    widest = array.shape.index(max(array.shape))
    beside = spot[:widest] + [(spot[widest] + 1) % array.shape[widest]] + spot[widest + 1:]
    return array.at[tuple(spot)].set(least).at[tuple(beside)].set(top_value)


def level_of(stream_key, dims, shards, smallest, largest):
    loudness = 1.0
    for axis_at, shards_of in shards:
        heights = jax.random.uniform(jax.random.fold_in(jax.random.fold_in(stream_key, 6), axis_at), (shards_of,), jnp.float32, smallest / len(shards), largest / len(shards))
        loudness = loudness * jnp.repeat(jnp.exp(heights), dims[axis_at] // shards_of).reshape((-1,) + (1,) * (len(dims) - 1 - axis_at))
    return loudness


def centred(rng, dims, deviation, most, cuts=(), held_as=jnp.bfloat16):
    drawn = jax.random.normal(rng, dims, jnp.float32) * deviation
    if len(cuts) > 0:
        drawn = level_of(rng, dims, cuts, -0.22, 0.18) * drawn
    return jnp.clip(drawn, min=-most, max=most).astype(held_as)


def setup_inputs(seed: int = 0, part: int = 0) -> dict:
    splits = jax.random.split(jax.random.key(seed), 23)
    part_keys = jax.random.split(jax.random.fold_in(splits[22], part), 23)
    grid_state = centred(part_keys[0], (GRID_NODES, VARS), 1.0, 6.0, ((0, 4),))
    mesh_state = centred(splits[1], (MESH_NODES, D), 1.0, 6.0, ((0, 4), (1, 4)))
    enc_rows = place_ends(jax.random.randint(splits[2], (N_GRID, N_GRID, CAP), 0, GRID_DEV), jax.random.fold_in(splits[2], 1), 0, GRID_DEV - 1).astype(jnp.int32)
    enc_targets = draw_enc_targets(jax.random.fold_in(splits[22], 71), part)
    mesh_senders = place_ends(jax.random.randint(splits[4], (MESH_EDGES,), 0, MESH_DEV + 2 * HALO), jax.random.fold_in(splits[4], 1), 0, (MESH_DEV + 2 * HALO) - 1).astype(jnp.int32)
    mesh_receivers = place_ends(jax.random.randint(splits[5], (MESH_EDGES,), 0, MESH_DEV), jax.random.fold_in(splits[5], 1), 0, MESH_DEV - 1).astype(jnp.int32)
    dec_rows = place_ends(jax.random.randint(splits[6], (N_GRID, N_GRID, CAP2), 0, MESH_DEV), jax.random.fold_in(splits[6], 1), 0, MESH_DEV - 1).astype(jnp.int32)
    dec_targets = draw_dec_targets(jax.random.fold_in(splits[22], 71), part)
    enc_grid_w = centred(splits[8], (VARS, D), VARS ** -0.5, 0.375, ((1, 4),))
    enc_mesh_w = centred(splits[9], (D, D), D ** -0.5, 0.25, ((1, 4),))
    enc_bias = centred(splits[10], (D,), 0.5, 3.0, ((0, 4),), jnp.float32)
    enc_out_w = centred(splits[11], (D, D), D ** -0.5, 0.25, ((0, 4),))
    enc_gain = jnp.clip(1.0 + 0.18 * jax.random.normal(splits[12], (D,), jnp.float32), 0.1, 1.9)
    proc_send_w = centred(splits[13], (PROC_LAYERS, D, D), D ** -0.5, 0.25, ((2, 4),))
    proc_recv_w = centred(splits[14], (PROC_LAYERS, D, D), D ** -0.5, 0.25, ((2, 4),))
    proc_bias = centred(splits[15], (PROC_LAYERS, D), 0.5, 3.0, ((1, 4),), jnp.float32)
    proc_out_w = centred(splits[16], (PROC_LAYERS, D, D), D ** -0.5, 0.25, ((1, 4),))
    proc_gain = jnp.clip(1.0 + 0.18 * jax.random.normal(splits[17], (PROC_LAYERS, D), jnp.float32), 0.1, 1.9)
    dec_mesh_w = centred(splits[18], (D, D), D ** -0.5, 0.25, ((1, 4),))
    dec_grid_w = centred(splits[19], (VARS, D), VARS ** -0.5, 0.375, ((1, 4),))
    dec_bias = centred(splits[20], (D,), 0.5, 3.0, ((0, 4),), jnp.float32)
    dec_out_w = centred(splits[21], (D, VARS), D ** -0.5, 0.25, ((0, 4),))
    return dict(grid_state=grid_state, mesh_state=mesh_state, enc_rows=enc_rows, enc_targets=enc_targets, mesh_senders=mesh_senders, mesh_receivers=mesh_receivers, dec_rows=dec_rows, dec_targets=dec_targets, enc_grid_w=enc_grid_w, enc_mesh_w=enc_mesh_w, enc_bias=enc_bias, enc_out_w=enc_out_w, enc_gain=enc_gain, proc_send_w=proc_send_w, proc_recv_w=proc_recv_w, proc_bias=proc_bias, proc_out_w=proc_out_w, proc_gain=proc_gain, dec_mesh_w=dec_mesh_w, dec_grid_w=dec_grid_w, dec_bias=dec_bias, dec_out_w=dec_out_w)


def normalize(values, scales):
    centre = lax.optimization_barrier(jnp.mean(values, axis=-1, keepdims=True))
    spread = lax.optimization_barrier(jnp.mean(values * values, axis=-1, keepdims=True)) - centre * centre
    return scales * ((values - centre) * lax.rsqrt(spread + 1e-05))

def reference(grid_state, mesh_state, enc_rows, enc_targets, mesh_senders, mesh_receivers, dec_rows, dec_targets, enc_grid_w, enc_mesh_w, enc_bias, enc_out_w, enc_gain, proc_send_w, proc_recv_w, proc_bias, proc_out_w, proc_gain, dec_mesh_w, dec_grid_w, dec_bias, dec_out_w):
    grid_total = N_GRID * GRID_DEV
    mesh_total = N_GRID * MESH_DEV
    owners = jnp.arange(N_GRID, dtype=jnp.int32)
    latent = mesh_state.astype(jnp.float32)
    grid_proj = jnp.dot(grid_state, enc_grid_w, preferred_element_type=jnp.float32).astype(jnp.bfloat16)
    mesh_proj = jnp.dot(mesh_state, enc_mesh_w, preferred_element_type=jnp.float32).astype(jnp.bfloat16)

    def encode(carry, inputs):
        rows, targets, source = inputs
        senders = rows.reshape(-1) + source * GRID_DEV
        receivers = jnp.where(targets < MESH_DEV, targets + owners[:, None] * MESH_DEV, mesh_total).reshape(-1).astype(jnp.int32)
        hidden = jax.nn.silu(grid_proj[senders].astype(jnp.float32) + mesh_proj[jnp.minimum(receivers, mesh_total - 1)].astype(jnp.float32) + enc_bias).astype(jnp.bfloat16)
        return (carry + jax.ops.segment_sum(hidden.astype(jnp.float32), receivers, num_segments=mesh_total + 1), None)
    summed, unused = lax.scan(encode, jnp.zeros((mesh_total + 1, D), jnp.float32), (enc_rows, enc_targets, owners))
    summed = summed[:mesh_total].astype(jnp.bfloat16)
    latent = latent + normalize(jnp.dot(summed, enc_out_w, preferred_element_type=jnp.float32), enc_gain)
    senders_all = mesh_senders.reshape(N_GRID, EDGE_DEV)
    receivers_all = mesh_receivers.reshape(N_GRID, EDGE_DEV)
    for layer_at in range(PROC_LAYERS):
        latent_bf = latent.astype(jnp.bfloat16)
        send_proj = jnp.dot(latent_bf, proc_send_w[layer_at], preferred_element_type=jnp.float32).astype(jnp.bfloat16)
        recv_proj = jnp.dot(latent_bf, proc_recv_w[layer_at], preferred_element_type=jnp.float32).astype(jnp.bfloat16)
        layer_bias = proc_bias[layer_at]

        def process(carry, inputs):
            senders, receivers, source = inputs
            glob_send = ((source * MESH_DEV + senders - HALO) % mesh_total).astype(jnp.int32)
            glob_recv = (source * MESH_DEV + receivers).astype(jnp.int32)
            hidden = jax.nn.silu(send_proj[glob_send].astype(jnp.float32) + recv_proj[glob_recv].astype(jnp.float32) + layer_bias).astype(jnp.bfloat16)
            return (carry + jax.ops.segment_sum(hidden.astype(jnp.float32), glob_recv, num_segments=mesh_total), None)
        summed, unused = lax.scan(process, jnp.zeros((mesh_total, D), jnp.float32), (senders_all, receivers_all, owners))
        latent = latent + normalize(jnp.dot(summed.astype(jnp.bfloat16), proc_out_w[layer_at], preferred_element_type=jnp.float32), proc_gain[layer_at])
    mesh_out = jnp.dot(latent.astype(jnp.bfloat16), dec_mesh_w, preferred_element_type=jnp.float32).astype(jnp.bfloat16)
    grid_query = jnp.dot(grid_state, dec_grid_w, preferred_element_type=jnp.float32).astype(jnp.bfloat16)

    def decode(carry, inputs):
        rows, targets, source = inputs
        senders = rows.reshape(-1) + source * MESH_DEV
        receivers = jnp.where(targets < GRID_DEV, targets + owners[:, None] * GRID_DEV, grid_total).reshape(-1).astype(jnp.int32)
        hidden = jax.nn.silu(mesh_out[senders].astype(jnp.float32) + grid_query[jnp.minimum(receivers, grid_total - 1)].astype(jnp.float32) + dec_bias).astype(jnp.bfloat16)
        return (carry + jax.ops.segment_sum(hidden.astype(jnp.float32), receivers, num_segments=grid_total + 1), None)
    summed, unused = lax.scan(decode, jnp.zeros((grid_total + 1, D), jnp.float32), (dec_rows, dec_targets, owners))
    summed = summed[:grid_total].astype(jnp.bfloat16)
    return grid_state.astype(jnp.float32) + jnp.dot(summed, dec_out_w, preferred_element_type=jnp.float32)
```

```python
import functools

import jax
import jax.numpy as jnp
from jax import lax
from jax.experimental import pallas as pl
from jax.experimental.pallas import tpu as pltpu
from jax.sharding import PartitionSpec as P

HALO = 64
BF = jnp.bfloat16
F32 = jnp.float32
EDGE_TILE = 128
EDGE_BLOCK = 512
MESH = pl.DeviceIdType.MESH


def repeat(count, body):
    if count <= 4:
        for i in range(count):
            body(i)
    else:

        def step(i, carry):
            body(i)
            return carry

        lax.fori_loop(0, count, step, 0)


def as_column(row):
    n = row.shape[1]
    diagonal = lax.broadcasted_iota(jnp.int32, (n, n), 0) == lax.broadcasted_iota(
        jnp.int32, (n, n), 1
    )
    spread = jnp.where(diagonal, jnp.broadcast_to(row.astype(F32), (n, n)), 0.0)
    return jnp.sum(spread, axis=1, keepdims=True)


def hits(index, count, offset):
    lanes = lax.broadcasted_iota(jnp.int32, (index.shape[0], count), 1) + offset
    wide = jnp.broadcast_to(index[:, :1], (index.shape[0], count))
    return jnp.where(wide == lanes.astype(F32), 1.0, 0.0).astype(BF)


def dot(a, b):
    return jnp.dot(a, b, preferred_element_type=F32)


def dot_t(a, b):
    return lax.dot_general(a, b, (((0,), (0,)), ((), ())), preferred_element_type=F32)


def silu(x):
    half = 0.5 * x
    return half + half * jnp.tanh(half)


def kernel(
    n_grid,
    n_feat,
    grid_state,
    mesh_state,
    enc_rows,
    enc_targets,
    senders,
    receivers,
    dec_rows,
    dec_targets,
    enc_grid_w,
    enc_mesh_w,
    enc_bias,
    enc_out_w,
    enc_gain,
    proc_send_w,
    proc_recv_w,
    proc_bias,
    proc_out_w,
    proc_gain,
    dec_mesh_w,
    dec_grid_w,
    dec_bias,
    dec_out_w,
    out,
    state_all,
    gain_all,
    out_w_all,
    dec_w_all,
    sums_all,
    dec_all,
    enc_out_slots,
    enc_out_index,
    dec_out_slots,
    dec_out_index,
    enc_in_slots,
    enc_in_index,
    dec_in_slots,
    dec_in_index,
    dec_pick,
    dec_query,
    dec_spread,
    gather_sel,
    scatter_sel,
    pre,
    table,
    halo,
    latent,
    latent_bf,
    send_sem,
    recv_sem,
):
    z = lax.axis_index("grid")
    f = lax.axis_index("feat")
    side = f + 1 - 2 * (f % 2)
    cross = (f + 2) % n_feat
    layers = proc_send_w.shape[0]
    nodes, part = mesh_state.shape
    grid_rows = grid_state.shape[0]
    cap, cap2 = enc_rows.shape[2], dec_rows.shape[2]
    edges = senders.shape[0] * EDGE_TILE
    sems = [0]
    sent = []

    def new_sem(count=1):
        sems[0] += count
        return sems[0] - count

    def send(src, dst, sem, where):
        return pltpu.make_async_remote_copy(
            src_ref=src,
            dst_ref=dst,
            send_sem=send_sem.at[sem],
            recv_sem=recv_sem.at[sem],
            device_id=where,
            device_id_type=MESH,
        )

    def columns(index):
        return pl.ds(pl.multiple_of(index * part, part), part)

    class Gather:
        def __init__(self, ref, by_rows, pieces):
            self.ref, self.by_rows = ref, by_rows
            size = (part if by_rows else ref.shape[0]) // pieces
            self.direct = send(self.at(f), self.at(f), new_sem(), {"feat": side})
            self.over, self.forward = [], []
            for k in range(pieces):
                here, there = self.at(f, k, size), self.at(cross, k, size)
                self.over.append(send(here, here, new_sem(), {"feat": cross}))
                self.forward.append(send(there, there, new_sem(), {"feat": side}))

        def at(self, index, k=0, size=None):
            if self.by_rows:
                size = part if size is None else size
                start = pl.multiple_of(index * part + k * size, size)
                return self.ref.at[pl.ds(start, size), :]
            size = self.ref.shape[0] if size is None else size
            return self.ref.at[pl.ds(k * size, size), columns(index)]

        def start(self):
            for copy in self.over:
                copy.start()
            self.direct.start()

        def middle(self):
            for over, forward in zip(self.over, self.forward):
                over.wait_recv()
                forward.start()

        def finish(self):
            self.direct.wait_recv()
            for forward in self.forward:
                forward.wait_recv()
            sent.extend([self.direct] + self.over + self.forward)

    class Exchange:
        def __init__(self, src, dst, size):
            self.src, self.dst, self.size = src, dst, size
            self.sem = new_sem(n_grid)

        def block(self, ref, index):
            return ref.at[pl.ds(pl.multiple_of(index * self.size, self.size), self.size), :]

        def copy(self, step):
            to = (z + step) % n_grid
            return send(
                self.block(self.src, to), self.block(self.dst, z), self.sem + step, {"grid": to}
            )

        def start(self):
            repeat(n_grid - 1, lambda i: self.copy(i + 1).start())
            self.block(self.dst, z)[...] = self.block(self.src, z)[...]

        def finish(self):
            repeat(n_grid - 1, lambda i: self.copy(i + 1).wait_recv())

        def end(self):
            repeat(n_grid - 1, lambda i: self.copy(i + 1).wait_send())

    barrier = pltpu.get_barrier_semaphore()
    for partner in (side, cross):
        pl.semaphore_signal(barrier, inc=1, device_id={"feat": partner}, device_id_type=MESH)
    repeat(
        n_grid - 1,
        lambda i: pl.semaphore_signal(
            barrier, inc=1, device_id={"grid": (z + i + 1) % n_grid}, device_id_type=MESH
        ),
    )

    state_all[:, columns(f)] = mesh_state[...]
    gain_all[:, columns(f)] = jnp.concatenate(
        [enc_gain[...], proc_gain[...], jnp.zeros((7 - layers, part), F32)], axis=0
    )
    out_w_all[0, columns(f), :] = enc_out_w[...]
    for layer in range(layers):
        out_w_all[1 + layer, columns(f), :] = proc_out_w[layer]
    dec_w_all[columns(f), :] = dec_out_w[...]

    state_gather = Gather(state_all, False, 2)
    gain_gather = Gather(gain_all, False, 1)
    weight_gathers = [Gather(out_w_all.at[i], True, 1) for i in range(1 + layers)]
    dec_weight_gather = Gather(dec_w_all, True, 1)
    sum_gathers = [Gather(sums_all.at[i], False, 4) for i in range(1 + layers)]
    dec_gather = Gather(dec_all, False, 2)
    enc_slots = Exchange(enc_out_slots, enc_in_slots, cap)
    enc_index = Exchange(enc_out_index, enc_in_index, cap)
    dec_slots = Exchange(dec_out_slots, dec_in_slots, cap2)
    dec_index = Exchange(dec_out_index, dec_in_index, cap2)

    pl.semaphore_wait(barrier, 2 + n_grid - 1)
    state_gather.start()

    def enc_send(b):
        rows = as_column(enc_rows[0, pl.ds(b, 1), :])
        picked = dot(hits(rows, grid_rows, 0), grid_state[...]).astype(BF)
        where = pl.ds(pl.multiple_of(b * cap, cap), cap)
        enc_out_slots[where, :] = dot(picked, enc_grid_w[...]).astype(BF)
        target = as_column(enc_targets[0, pl.ds(b, 1), :])
        enc_out_index[where, :] = jnp.broadcast_to(target, (cap, 128))

    repeat(n_grid, enc_send)
    enc_slots.start()
    enc_index.start()
    gain_gather.start()
    weight_gathers[0].start()

    def dec_prepare(b):
        where = pl.ds(pl.multiple_of(b * cap2, cap2), cap2)
        target = as_column(dec_targets[0, pl.ds(b, 1), :])
        dec_out_index[where, :] = jnp.broadcast_to(target, (cap2, 128))
        dec_pick[where, :] = hits(as_column(dec_rows[0, pl.ds(b, 1), :]), nodes, 0)

    repeat(n_grid, dec_prepare)
    dec_index.start()
    state_gather.middle()

    def edge_tile(j):
        where = pl.ds(pl.multiple_of(j * EDGE_TILE, EDGE_TILE), EDGE_TILE)
        to_row = receivers[pl.ds(j, 1), :]
        sender, receiver = as_column(senders[pl.ds(j, 1), :]), as_column(to_row)
        gather_sel[where, :nodes] = hits(sender, nodes, HALO)
        gather_sel[where, nodes : 2 * nodes] = hits(receiver, nodes, 0)
        lane = lax.broadcasted_iota(jnp.int32, (EDGE_TILE, 2 * HALO), 1)
        ends = jnp.where(lane < HALO, lane, lane + nodes).astype(F32)
        gather_sel[where, 2 * nodes :] = jnp.where(
            jnp.broadcast_to(sender, ends.shape) == ends, 1.0, 0.0
        ).astype(BF)
        row = lax.broadcasted_iota(jnp.int32, (nodes, EDGE_TILE), 0)
        scatter_sel[:, where] = jnp.where(
            jnp.broadcast_to(to_row, row.shape) == row, 1.0, 0.0
        ).astype(BF)

    def edge_tiles(first, last):
        lax.fori_loop(first, last, lambda j, c: (edge_tile(j), c)[1], 0)

    tiles = edges // EDGE_TILE
    edge_tiles(0, tiles // 2)
    gain_gather.middle()
    weight_gathers[0].middle()

    state_gather.finish()
    mesh_proj = dot(state_all[...], enc_mesh_w[...]).astype(BF)
    enc_slots.finish()
    enc_index.finish()

    total = jnp.zeros((nodes, part), F32)
    chunk = 4 * cap
    for i in range(n_grid // 4):
        where = pl.ds(i * chunk, chunk)
        select = hits(enc_in_index[where, :], nodes, 0)
        before = enc_in_slots[where, :].astype(F32) + dot(select, mesh_proj) + enc_bias[...]
        total += dot_t(select, silu(before).astype(BF))
    sums_all[0, :, columns(f)] = total.astype(BF)
    sum_gathers[0].start()
    edge_tiles(tiles // 2, tiles)

    block = 128

    def update(step):
        gather = sum_gathers[step]
        gather.middle()
        if step == 0:
            gain_gather.finish()
        weight_gathers[step].finish()
        gather.finish()
        for i in range(nodes // block):
            rows = slice(i * block, (i + 1) * block)
            u = dot(sums_all[step, rows, :], out_w_all[step])
            centre = jnp.mean(u, axis=1, keepdims=True)
            spread = jnp.mean(u * u, axis=1, keepdims=True) - centre * centre
            held = state_all[rows, :].astype(F32) if step == 0 else latent[rows, :]
            held += gain_all[step : step + 1, :] * ((u - centre) * lax.rsqrt(spread + 1e-05))
            latent[rows, :] = held
            latent_bf[rows, :] = held.astype(BF)

    update(0)
    right, left = (z + 1) % n_grid, (z + n_grid - 1) % n_grid
    for layer in range(layers):
        table[layer, :nodes, :] = dot(latent_bf[...], proc_send_w[layer]).astype(BF)
        up = send(
            table.at[layer, pl.ds(nodes - HALO, HALO), :],
            halo.at[layer, pl.ds(0, HALO), :],
            new_sem(),
            {"grid": right},
        )
        down = send(
            table.at[layer, pl.ds(0, HALO), :],
            halo.at[layer, pl.ds(HALO, HALO), :],
            new_sem(),
            {"grid": left},
        )
        up.start()
        down.start()
        weight_gathers[1 + layer].start()
        if layer == layers - 1:
            dec_weight_gather.start()
        table[layer, nodes:, :] = dot(latent_bf[...], proc_recv_w[layer]).astype(BF)
        for i in range(edges // EDGE_BLOCK):
            rows = slice(i * EDGE_BLOCK, (i + 1) * EDGE_BLOCK)
            pre[rows, :] = dot(gather_sel[rows, : 2 * nodes], table[layer])
        up.wait_recv()
        down.wait_recv()
        weight_gathers[1 + layer].middle()
        if layer == layers - 1:
            dec_weight_gather.middle()
        total = jnp.zeros((nodes, part), F32)
        for i in range(edges // EDGE_BLOCK):
            rows = slice(i * EDGE_BLOCK, (i + 1) * EDGE_BLOCK)
            before = pre[rows, :] + dot(gather_sel[rows, 2 * nodes :], halo[layer])
            hidden = silu(before + proc_bias[layer : layer + 1, :]).astype(BF)
            total += dot(scatter_sel[:, rows], hidden)
        sums_all[1 + layer, :, columns(f)] = total.astype(BF)
        sum_gathers[1 + layer].start()
        sent.extend([up, down])
        if layer == 0:
            dec_index.finish()
            query = dot(grid_state[...], dec_grid_w[...]).astype(BF)
            quarter = grid_rows // n_feat
            for i in range(n_grid // 4):
                where = pl.ds(i * 4 * cap2, 4 * cap2)
                targets = dec_in_index[where, :]
                dec_query[where, :] = dot(hits(targets, grid_rows, 0), query) + dec_bias[...]
                dec_spread[where, :] = hits(targets, quarter, f * quarter)
        update(1 + layer)

    mesh_out = dot(latent_bf[...], dec_mesh_w[...]).astype(BF)
    for i in range(n_grid // 4):
        where = pl.ds(i * 4 * cap2, 4 * cap2)
        dec_out_slots[where, :] = dot(dec_pick[where, :], mesh_out).astype(BF)
    dec_slots.start()
    dec_slots.finish()
    for i in range(n_grid // 4):
        where = pl.ds(i * 4 * cap2, 4 * cap2)
        before = dec_in_slots[where, :].astype(F32) + dec_query[where, :]
        dec_all[where, columns(f)] = silu(before).astype(BF)
    dec_gather.start()
    dec_weight_gather.finish()
    dec_gather.middle()
    dec_gather.finish()
    quarter = grid_rows // n_feat
    total = jnp.zeros((quarter, part * n_feat), F32)
    for i in range(n_grid // 4):
        where = pl.ds(i * 4 * cap2, 4 * cap2)
        total += dot_t(dec_spread[where, :], dec_all[where, :])
    own = grid_state[pl.ds(pl.multiple_of(f * quarter, quarter), quarter), :]
    out[...] = own.astype(F32) + dot(total.astype(BF), dec_w_all[...])

    for copy in sent:
        copy.wait_send()
    for exchange in (enc_slots, enc_index, dec_slots, dec_index):
        exchange.end()


def local(
    grid_state,
    mesh_state,
    enc_rows,
    enc_targets,
    mesh_senders,
    mesh_receivers,
    dec_rows,
    dec_targets,
    enc_grid_w,
    enc_mesh_w,
    enc_bias,
    enc_out_w,
    enc_gain,
    proc_send_w,
    proc_recv_w,
    proc_bias,
    proc_out_w,
    proc_gain,
    dec_mesh_w,
    dec_grid_w,
    dec_bias,
    dec_out_w,
):
    n_grid, n_feat = lax.axis_size("grid"), lax.axis_size("feat")
    layers = proc_send_w.shape[0]
    nodes, part = mesh_state.shape
    width = part * n_feat
    grid_rows, variables = grid_state.shape
    enc_total = n_grid * enc_rows.shape[2]
    dec_total = n_grid * dec_rows.shape[2]
    edges = mesh_senders.shape[0]
    quarter = grid_rows // n_feat
    sems = 9 * 12 + 2 * layers + 4 * n_grid
    args = (
        grid_state,
        mesh_state,
        enc_rows,
        enc_targets,
        mesh_senders.reshape(-1, EDGE_TILE),
        mesh_receivers.reshape(-1, EDGE_TILE),
        dec_rows,
        dec_targets,
        enc_grid_w,
        enc_mesh_w,
        enc_bias.reshape(1, -1),
        enc_out_w,
        enc_gain.reshape(1, -1),
        proc_send_w,
        proc_recv_w,
        proc_bias,
        proc_out_w,
        proc_gain,
        dec_mesh_w,
        dec_grid_w,
        dec_bias.reshape(1, -1),
        dec_out_w,
    )
    return pl.pallas_call(
        functools.partial(kernel, n_grid, n_feat),
        out_shape=jax.ShapeDtypeStruct((quarter, variables), F32),
        in_specs=[pl.BlockSpec(memory_space=pltpu.VMEM)] * len(args),
        out_specs=pl.BlockSpec(memory_space=pltpu.VMEM),
        scratch_shapes=[
            pltpu.VMEM((nodes, width), BF),
            pltpu.VMEM((8, width), F32),
            pltpu.VMEM((1 + layers, width, width), BF),
            pltpu.VMEM((width, variables), BF),
            pltpu.VMEM((1 + layers, nodes, width), BF),
            pltpu.VMEM((dec_total, width), BF),
            pltpu.VMEM((enc_total, part), BF),
            pltpu.VMEM((enc_total, 128), F32),
            pltpu.VMEM((dec_total, part), BF),
            pltpu.VMEM((dec_total, 128), F32),
            pltpu.VMEM((enc_total, part), BF),
            pltpu.VMEM((enc_total, 128), F32),
            pltpu.VMEM((dec_total, part), BF),
            pltpu.VMEM((dec_total, 128), F32),
            pltpu.VMEM((dec_total, nodes), BF),
            pltpu.VMEM((dec_total, part), F32),
            pltpu.VMEM((dec_total, quarter), BF),
            pltpu.VMEM((edges, 2 * nodes + 2 * HALO), BF),
            pltpu.VMEM((nodes, edges), BF),
            pltpu.VMEM((edges, part), F32),
            pltpu.VMEM((layers, 2 * nodes, part), BF),
            pltpu.VMEM((layers, 2 * HALO, part), BF),
            pltpu.VMEM((nodes, width), F32),
            pltpu.VMEM((nodes, width), BF),
            pltpu.SemaphoreType.DMA((sems,)),
            pltpu.SemaphoreType.DMA((sems,)),
        ],
        compiler_params=pltpu.CompilerParams(
            collective_id=0, has_side_effects=True, vmem_limit_bytes=56 * 1024 * 1024
        ),
    )(*args)


def solution(mesh):
    in_specs = (
        P(("groups", "grid"), None),
        P("grid", "feat"),
        P("grid", None, None),
        P("grid", None, None),
        P("grid"),
        P("grid"),
        P("grid", None, None),
        P("grid", None, None),
        P(None, "feat"),
        P(None, "feat"),
        P("feat"),
        P("feat", None),
        P("feat"),
        P(None, None, "feat"),
        P(None, None, "feat"),
        P(None, "feat"),
        P(None, "feat", None),
        P(None, "feat"),
        P(None, "feat"),
        P(None, "feat"),
        P("feat"),
        P("feat", None),
    )
    out_specs = P(("groups", "grid", "feat"), None)
    return jax.shard_map(local, mesh=mesh, in_specs=in_specs, out_specs=out_specs, check_vma=False)
```

```python
import functools

import jax
import jax.numpy as jnp
from jax import lax
from jax.experimental import pallas as pl
from jax.experimental.pallas import tpu as pltpu
from jax.sharding import PartitionSpec as P

HALO = 64
BF = jnp.bfloat16
F32 = jnp.float32
EDGE_TILE = 128
EDGE_BLOCK = 512
MESH = pl.DeviceIdType.MESH


def repeat(count, body):
    if count <= 4:
        for i in range(count):
            body(i)
    else:

        def step(i, carry):
            body(i)
            return carry

        lax.fori_loop(0, count, step, 0)


def as_column(row):
    n = row.shape[1]
    diagonal = lax.broadcasted_iota(jnp.int32, (n, n), 0) == lax.broadcasted_iota(
        jnp.int32, (n, n), 1
    )
    spread = jnp.where(diagonal, jnp.broadcast_to(row.astype(F32), (n, n)), 0.0)
    return jnp.sum(spread, axis=1, keepdims=True)


def hits(index, count, offset):
    lanes = lax.broadcasted_iota(jnp.int32, (index.shape[0], count), 1) + offset
    wide = jnp.broadcast_to(index[:, :1], (index.shape[0], count))
    return jnp.where(wide == lanes.astype(F32), 1.0, 0.0).astype(BF)


def dot(a, b):
    return jnp.dot(a, b, preferred_element_type=F32)


def dot_t(a, b):
    return lax.dot_general(a, b, (((0,), (0,)), ((), ())), preferred_element_type=F32)


def dot_n(a, b):
    return lax.dot_general(a, b, (((1,), (1,)), ((), ())), preferred_element_type=F32)


def silu(x):
    half = 0.5 * x
    return half + half * jnp.tanh(half)


def kernel(
    n_grid,
    n_feat,
    grid_state,
    mesh_state,
    enc_rows,
    enc_targets,
    senders,
    receivers,
    dec_rows,
    dec_targets,
    enc_grid_w,
    enc_mesh_w,
    enc_bias,
    enc_out_w,
    enc_gain,
    proc_send_w,
    proc_recv_w,
    proc_bias,
    proc_out_w,
    proc_gain,
    dec_mesh_w,
    dec_grid_w,
    dec_bias,
    dec_out_w,
    out,
    state_all,
    gain_all,
    out_w_all,
    dec_w_all,
    sums_all,
    dec_all,
    enc_out_slots,
    enc_out_index,
    dec_out_slots,
    dec_out_index,
    enc_in_slots,
    enc_in_index,
    dec_in_slots,
    dec_in_index,
    dec_pick,
    dec_query,
    dec_spread,
    gather_sel,
    scatter_sel,
    pre,
    table,
    halo,
    latent,
    latent_bf,
    send_sem,
    recv_sem,
):
    z = lax.axis_index("grid")
    f = lax.axis_index("feat")
    side = f + 1 - 2 * (f % 2)
    cross = (f + 2) % n_feat
    layers = proc_send_w.shape[0]
    nodes, part = mesh_state.shape
    variables, grid_rows = grid_state.shape
    cap, cap2 = enc_rows.shape[2], dec_rows.shape[2]
    edges = senders.shape[0] * EDGE_TILE
    sems = [0]
    sent = []

    def new_sem(count=1):
        sems[0] += count
        return sems[0] - count

    def send(src, dst, sem, where):
        return pltpu.make_async_remote_copy(
            src_ref=src,
            dst_ref=dst,
            send_sem=send_sem.at[sem],
            recv_sem=recv_sem.at[sem],
            device_id=where,
            device_id_type=MESH,
        )

    def columns(index):
        return pl.ds(pl.multiple_of(index * part, part), part)

    class Gather:
        def __init__(self, ref, by_rows, pieces):
            self.ref, self.by_rows = ref, by_rows
            size = (part if by_rows else ref.shape[0]) // pieces
            self.direct = send(self.at(f), self.at(f), new_sem(), {"feat": side})
            self.over, self.forward = [], []
            for k in range(pieces):
                here, there = self.at(f, k, size), self.at(cross, k, size)
                self.over.append(send(here, here, new_sem(), {"feat": cross}))
                self.forward.append(send(there, there, new_sem(), {"feat": side}))

        def at(self, index, k=0, size=None):
            if self.by_rows:
                size = part if size is None else size
                start = pl.multiple_of(index * part + k * size, size)
                return self.ref.at[pl.ds(start, size), :]
            size = self.ref.shape[0] if size is None else size
            return self.ref.at[pl.ds(k * size, size), columns(index)]

        def start(self):
            for copy in self.over:
                copy.start()
            self.direct.start()

        def middle(self):
            for over, forward in zip(self.over, self.forward):
                over.wait_recv()
                forward.start()

        def finish(self):
            self.direct.wait_recv()
            for forward in self.forward:
                forward.wait_recv()
            sent.extend([self.direct] + self.over + self.forward)

    class Exchange:
        def __init__(self, src, dst, size):
            self.src, self.dst, self.size = src, dst, size
            self.sem = new_sem(n_grid)

        def block(self, ref, index):
            return ref.at[pl.ds(pl.multiple_of(index * self.size, self.size), self.size), :]

        def copy(self, step):
            to = (z + step) % n_grid
            return send(
                self.block(self.src, to), self.block(self.dst, z), self.sem + step, {"grid": to}
            )

        def start(self):
            repeat(n_grid - 1, lambda i: self.copy(i + 1).start())
            self.block(self.dst, z)[...] = self.block(self.src, z)[...]

        def finish(self):
            repeat(n_grid - 1, lambda i: self.copy(i + 1).wait_recv())

        def end(self):
            repeat(n_grid - 1, lambda i: self.copy(i + 1).wait_send())

    barrier = pltpu.get_barrier_semaphore()
    for partner in (side, cross):
        pl.semaphore_signal(barrier, inc=1, device_id={"feat": partner}, device_id_type=MESH)
    repeat(
        n_grid - 1,
        lambda i: pl.semaphore_signal(
            barrier, inc=1, device_id={"grid": (z + i + 1) % n_grid}, device_id_type=MESH
        ),
    )

    state_all[:, columns(f)] = mesh_state[...]
    gain_all[:, columns(f)] = jnp.concatenate(
        [enc_gain[...], proc_gain[...], jnp.zeros((7 - layers, part), F32)], axis=0
    )
    out_w_all[0, columns(f), :] = enc_out_w[...]
    for layer in range(layers):
        out_w_all[1 + layer, columns(f), :] = proc_out_w[layer]
    dec_w_all[:, columns(f)] = jnp.zeros((dec_w_all.shape[0], part), BF)
    dec_w_all[:variables, columns(f)] = dec_out_w[...]

    block = 128
    state_gather = Gather(state_all, False, 2)
    gain_gather = Gather(gain_all, False, 1)
    weight_gathers = [Gather(out_w_all.at[i], True, 1) for i in range(1 + layers)]
    dec_weight_gather = Gather(dec_w_all, False, 1)
    sum_gathers = [Gather(sums_all.at[i], False, nodes // block) for i in range(1 + layers)]
    dec_gather = Gather(dec_all, False, 2)
    enc_slots = Exchange(enc_out_slots, enc_in_slots, cap)
    enc_index = Exchange(enc_out_index, enc_in_index, cap)
    dec_slots = Exchange(dec_out_slots, dec_in_slots, cap2)
    dec_index = Exchange(dec_out_index, dec_in_index, cap2)

    pl.semaphore_wait(barrier, 2 + n_grid - 1)
    state_gather.start()

    grid_proj = dot_t(grid_state[...], enc_grid_w[...]).astype(BF)
    for i in range(n_grid // 4):
        parts = range(4 * i, 4 * i + 4)
        where = pl.ds(i * 4 * cap, 4 * cap)
        rows = jnp.concatenate([as_column(enc_rows[0, b : b + 1, :]) for b in parts], axis=0)
        enc_out_slots[where, :] = dot(hits(rows, grid_rows, 0), grid_proj).astype(BF)
        target = jnp.concatenate([as_column(enc_targets[0, b : b + 1, :]) for b in parts], axis=0)
        enc_out_index[where, :] = jnp.broadcast_to(target, (4 * cap, 128))
    enc_slots.start()
    enc_index.start()
    gain_gather.start()
    weight_gathers[0].start()

    def dec_prepare(b):
        where = pl.ds(pl.multiple_of(b * cap2, cap2), cap2)
        target = as_column(dec_targets[0, pl.ds(b, 1), :])
        dec_out_index[where, :] = jnp.broadcast_to(target, (cap2, 128))
        dec_pick[where, :] = hits(as_column(dec_rows[0, pl.ds(b, 1), :]), nodes, 0)

    repeat(n_grid, dec_prepare)
    dec_index.start()
    state_gather.middle()

    def edge_tile(j):
        where = pl.ds(pl.multiple_of(j * EDGE_TILE, EDGE_TILE), EDGE_TILE)
        to_row = receivers[pl.ds(j, 1), :]
        sender, receiver = as_column(senders[pl.ds(j, 1), :]), as_column(to_row)
        gather_sel[where, :nodes] = hits(sender, nodes, HALO)
        gather_sel[where, nodes : 2 * nodes] = hits(receiver, nodes, 0)
        lane = lax.broadcasted_iota(jnp.int32, (EDGE_TILE, 2 * HALO), 1)
        ends = jnp.where(lane < HALO, lane, lane + nodes).astype(F32)
        gather_sel[where, 2 * nodes :] = jnp.where(
            jnp.broadcast_to(sender, ends.shape) == ends, 1.0, 0.0
        ).astype(BF)
        row = lax.broadcasted_iota(jnp.int32, (nodes, EDGE_TILE), 0)
        scatter_sel[:, where] = jnp.where(
            jnp.broadcast_to(to_row, row.shape) == row, 1.0, 0.0
        ).astype(BF)

    def edge_tiles(first, last):
        lax.fori_loop(first, last, lambda j, c: (edge_tile(j), c)[1], 0)

    tiles = edges // EDGE_TILE
    edge_tiles(0, tiles // 2)
    gain_gather.middle()
    weight_gathers[0].middle()

    state_gather.finish()
    mesh_proj = dot(state_all[...], enc_mesh_w[...]).astype(BF)
    enc_slots.finish()
    enc_index.finish()

    total = jnp.zeros((nodes, part), F32)
    chunk = 4 * cap
    for i in range(n_grid // 4):
        where = pl.ds(i * chunk, chunk)
        select = hits(enc_in_index[where, :], nodes, 0)
        before = enc_in_slots[where, :].astype(F32) + dot(select, mesh_proj) + enc_bias[...]
        total += dot_t(select, silu(before).astype(BF))
    sums_all[0, :, columns(f)] = total.astype(BF)
    sum_gathers[0].start()
    edge_tiles(tiles // 2, tiles)

    def update(step):
        gather = sum_gathers[step]
        gather.middle()
        if step == 0:
            gain_gather.finish()
        weight_gathers[step].finish()
        gather.direct.wait_recv()
        for i in range(nodes // block):
            rows = slice(i * block, (i + 1) * block)
            gather.forward[i].wait_recv()
            u = dot(sums_all[step, rows, :], out_w_all[step])
            centre = jnp.mean(u, axis=1, keepdims=True)
            spread = jnp.mean(u * u, axis=1, keepdims=True) - centre * centre
            held = state_all[rows, :].astype(F32) if step == 0 else latent[rows, :]
            held += gain_all[step : step + 1, :] * ((u - centre) * lax.rsqrt(spread + 1e-05))
            latent[rows, :] = held
            latent_bf[rows, :] = held.astype(BF)
        sent.extend([gather.direct] + gather.over + gather.forward)

    update(0)
    right, left = (z + 1) % n_grid, (z + n_grid - 1) % n_grid
    for layer in range(layers):
        table[layer, :nodes, :] = dot(latent_bf[...], proc_send_w[layer]).astype(BF)
        up = send(
            table.at[layer, pl.ds(nodes - HALO, HALO), :],
            halo.at[layer, pl.ds(0, HALO), :],
            new_sem(),
            {"grid": right},
        )
        down = send(
            table.at[layer, pl.ds(0, HALO), :],
            halo.at[layer, pl.ds(HALO, HALO), :],
            new_sem(),
            {"grid": left},
        )
        up.start()
        down.start()
        weight_gathers[1 + layer].start()
        if layer == layers - 1:
            dec_weight_gather.start()
        table[layer, nodes:, :] = dot(latent_bf[...], proc_recv_w[layer]).astype(BF)
        for i in range(edges // EDGE_BLOCK):
            rows = slice(i * EDGE_BLOCK, (i + 1) * EDGE_BLOCK)
            pre[rows, :] = dot(gather_sel[rows, : 2 * nodes], table[layer])
        up.wait_recv()
        down.wait_recv()
        weight_gathers[1 + layer].middle()
        if layer == layers - 1:
            dec_weight_gather.middle()
        total = jnp.zeros((nodes, part), F32)
        for i in range(edges // EDGE_BLOCK):
            rows = slice(i * EDGE_BLOCK, (i + 1) * EDGE_BLOCK)
            before = pre[rows, :] + dot(gather_sel[rows, 2 * nodes :], halo[layer])
            hidden = silu(before + proc_bias[layer : layer + 1, :]).astype(BF)
            total += dot(scatter_sel[:, rows], hidden)
        sums_all[1 + layer, :, columns(f)] = total.astype(BF)
        sum_gathers[1 + layer].start()
        sent.extend([up, down])
        if layer == 0:
            dec_index.finish()
            query = dot_t(grid_state[...], dec_grid_w[...]).astype(BF)
            quarter = grid_rows // n_feat
            for i in range(n_grid // 4):
                where = pl.ds(i * 4 * cap2, 4 * cap2)
                targets = dec_in_index[where, :]
                dec_query[where, :] = dot(hits(targets, grid_rows, 0), query) + dec_bias[...]
                dec_spread[where, :] = hits(targets, quarter, f * quarter)
        update(1 + layer)

    mesh_out = dot(latent_bf[...], dec_mesh_w[...]).astype(BF)
    for i in range(n_grid // 4):
        where = pl.ds(i * 4 * cap2, 4 * cap2)
        dec_out_slots[where, :] = dot(dec_pick[where, :], mesh_out).astype(BF)
    dec_slots.start()
    dec_slots.finish()
    for i in range(n_grid // 4):
        where = pl.ds(i * 4 * cap2, 4 * cap2)
        before = dec_in_slots[where, :].astype(F32) + dec_query[where, :]
        dec_all[where, columns(f)] = silu(before).astype(BF)
    dec_gather.start()
    dec_weight_gather.finish()
    dec_gather.middle()
    dec_gather.finish()
    quarter = grid_rows // n_feat
    total = jnp.zeros((quarter, part * n_feat), F32)
    for i in range(n_grid // 4):
        where = pl.ds(i * 4 * cap2, 4 * cap2)
        total += dot_t(dec_spread[where, :], dec_all[where, :])
    own = grid_state[:, pl.ds(pl.multiple_of(f * quarter, quarter), quarter)]
    added = dot_n(dec_w_all[...], total.astype(BF))
    out[...] = own.astype(F32) + added[:variables, :]

    for copy in sent:
        copy.wait_send()
    for exchange in (enc_slots, enc_index, dec_slots, dec_index):
        exchange.end()


def local(
    grid_state,
    mesh_state,
    enc_rows,
    enc_targets,
    mesh_senders,
    mesh_receivers,
    dec_rows,
    dec_targets,
    enc_grid_w,
    enc_mesh_w,
    enc_bias,
    enc_out_w,
    enc_gain,
    proc_send_w,
    proc_recv_w,
    proc_bias,
    proc_out_w,
    proc_gain,
    dec_mesh_w,
    dec_grid_w,
    dec_bias,
    dec_out_w,
):
    n_grid, n_feat = lax.axis_size("grid"), lax.axis_size("feat")
    layers = proc_send_w.shape[0]
    nodes, part = mesh_state.shape
    width = part * n_feat
    grid_rows, variables = grid_state.shape
    enc_total = n_grid * enc_rows.shape[2]
    dec_total = n_grid * dec_rows.shape[2]
    edges = mesh_senders.shape[0]
    quarter = grid_rows // n_feat
    sems = 9 * 12 + 2 * layers + 4 * n_grid
    args = (
        grid_state.T,
        mesh_state,
        enc_rows,
        enc_targets,
        mesh_senders.reshape(-1, EDGE_TILE),
        mesh_receivers.reshape(-1, EDGE_TILE),
        dec_rows,
        dec_targets,
        enc_grid_w,
        enc_mesh_w,
        enc_bias.reshape(1, -1),
        enc_out_w,
        enc_gain.reshape(1, -1),
        proc_send_w,
        proc_recv_w,
        proc_bias,
        proc_out_w,
        proc_gain,
        dec_mesh_w,
        dec_grid_w,
        dec_bias.reshape(1, -1),
        dec_out_w.T,
    )
    return pl.pallas_call(
        functools.partial(kernel, n_grid, n_feat),
        out_shape=jax.ShapeDtypeStruct((variables, quarter), F32),
        in_specs=[pl.BlockSpec(memory_space=pltpu.VMEM)] * len(args),
        out_specs=pl.BlockSpec(memory_space=pltpu.VMEM),
        scratch_shapes=[
            pltpu.VMEM((nodes, width), BF),
            pltpu.VMEM((8, width), F32),
            pltpu.VMEM((1 + layers, width, width), BF),
            pltpu.VMEM((-(-variables // 16) * 16, width), BF),
            pltpu.VMEM((1 + layers, nodes, width), BF),
            pltpu.VMEM((dec_total, width), BF),
            pltpu.VMEM((enc_total, part), BF),
            pltpu.VMEM((enc_total, 128), F32),
            pltpu.VMEM((dec_total, part), BF),
            pltpu.VMEM((dec_total, 128), F32),
            pltpu.VMEM((enc_total, part), BF),
            pltpu.VMEM((enc_total, 128), F32),
            pltpu.VMEM((dec_total, part), BF),
            pltpu.VMEM((dec_total, 128), F32),
            pltpu.VMEM((dec_total, nodes), BF),
            pltpu.VMEM((dec_total, part), F32),
            pltpu.VMEM((dec_total, quarter), BF),
            pltpu.VMEM((edges, 2 * nodes + 2 * HALO), BF),
            pltpu.VMEM((nodes, edges), BF),
            pltpu.VMEM((edges, part), F32),
            pltpu.VMEM((layers, 2 * nodes, part), BF),
            pltpu.VMEM((layers, 2 * HALO, part), BF),
            pltpu.VMEM((nodes, width), F32),
            pltpu.VMEM((nodes, width), BF),
            pltpu.SemaphoreType.DMA((sems,)),
            pltpu.SemaphoreType.DMA((sems,)),
        ],
        compiler_params=pltpu.CompilerParams(
            collective_id=0, has_side_effects=True, vmem_limit_bytes=56 * 1024 * 1024
        ),
    )(*args).T


def solution(mesh):
    in_specs = (
        P(("groups", "grid"), None),
        P("grid", "feat"),
        P("grid", None, None),
        P("grid", None, None),
        P("grid"),
        P("grid"),
        P("grid", None, None),
        P("grid", None, None),
        P(None, "feat"),
        P(None, "feat"),
        P("feat"),
        P("feat", None),
        P("feat"),
        P(None, None, "feat"),
        P(None, None, "feat"),
        P(None, "feat"),
        P(None, "feat", None),
        P(None, "feat"),
        P(None, "feat"),
        P(None, "feat"),
        P("feat"),
        P("feat", None),
    )
    out_specs = P(("groups", "grid", "feat"), None)
    return jax.shard_map(local, mesh=mesh, in_specs=in_specs, out_specs=out_specs, check_vma=False)
```

```python
import functools

import jax
import jax.numpy as jnp
from jax import lax
from jax.experimental import pallas as pl
from jax.experimental.pallas import tpu as pltpu
from jax.sharding import PartitionSpec as P

HALO = 64
BF = jnp.bfloat16
F32 = jnp.float32
EDGE_TILE = 128
EDGE_BLOCK = 512
MESH = pl.DeviceIdType.MESH


def repeat(count, body):
    if count <= 4:
        for i in range(count):
            body(i)
    else:

        def step(i, carry):
            body(i)
            return carry

        lax.fori_loop(0, count, step, 0)


def as_column(row):
    n = row.shape[1]
    diagonal = lax.broadcasted_iota(jnp.int32, (n, n), 0) == lax.broadcasted_iota(
        jnp.int32, (n, n), 1
    )
    spread = jnp.where(diagonal, jnp.broadcast_to(row.astype(F32), (n, n)), 0.0)
    return jnp.sum(spread, axis=1, keepdims=True)


def hits(index, count, offset):
    lanes = lax.broadcasted_iota(jnp.int32, (index.shape[0], count), 1) + offset
    wide = jnp.broadcast_to(index[:, :1], (index.shape[0], count))
    return jnp.where(wide == lanes.astype(F32), 1.0, 0.0).astype(BF)


def dot(a, b):
    return jnp.dot(a, b, preferred_element_type=F32)


def dot_t(a, b):
    return lax.dot_general(a, b, (((0,), (0,)), ((), ())), preferred_element_type=F32)


def dot_n(a, b):
    return lax.dot_general(a, b, (((1,), (1,)), ((), ())), preferred_element_type=F32)


def silu(x):
    half = 0.5 * x
    return half + half * jnp.tanh(half)


def kernel(
    n_grid,
    n_feat,
    grid_state,
    mesh_state,
    enc_rows,
    enc_targets,
    senders,
    receivers,
    dec_rows,
    dec_targets,
    enc_grid_w,
    enc_mesh_w,
    enc_bias,
    enc_out_w,
    enc_gain,
    proc_send_w,
    proc_recv_w,
    proc_bias,
    proc_out_w,
    proc_gain,
    dec_mesh_w,
    dec_grid_w,
    dec_bias,
    dec_out_w,
    out,
    state_all,
    gain_all,
    out_w_all,
    dec_w_all,
    sums_all,
    dec_all,
    enc_out_slots,
    enc_out_index,
    dec_out_slots,
    dec_out_index,
    enc_in_slots,
    enc_in_index,
    dec_in_slots,
    dec_in_index,
    dec_pick,
    dec_query,
    dec_spread,
    gather_sel,
    scatter_sel,
    pre,
    table,
    halo,
    latent,
    latent_bf,
    send_sem,
    recv_sem,
):
    z = lax.axis_index("grid")
    f = lax.axis_index("feat")
    side = f + 1 - 2 * (f % 2)
    cross = (f + 2) % n_feat
    layers = proc_send_w.shape[0]
    nodes, part = mesh_state.shape
    variables, grid_rows = grid_state.shape
    cap, cap2 = enc_rows.shape[2], dec_rows.shape[2]
    edges = senders.shape[0] * EDGE_TILE
    sems = [0]
    sent = []

    def new_sem(count=1):
        sems[0] += count
        return sems[0] - count

    def send(src, dst, sem, where):
        return pltpu.make_async_remote_copy(
            src_ref=src,
            dst_ref=dst,
            send_sem=send_sem.at[sem],
            recv_sem=recv_sem.at[sem],
            device_id=where,
            device_id_type=MESH,
        )

    def columns(index):
        return pl.ds(pl.multiple_of(index * part, part), part)

    class Gather:
        def __init__(self, ref, by_rows, pieces):
            self.ref, self.by_rows = ref, by_rows
            size = (part if by_rows else ref.shape[0]) // pieces
            self.direct = send(self.at(f), self.at(f), new_sem(), {"feat": side})
            self.over, self.forward = [], []
            for k in range(pieces):
                here, there = self.at(f, k, size), self.at(cross, k, size)
                self.over.append(send(here, here, new_sem(), {"feat": cross}))
                self.forward.append(send(there, there, new_sem(), {"feat": side}))

        def at(self, index, k=0, size=None):
            if self.by_rows:
                size = part if size is None else size
                start = pl.multiple_of(index * part + k * size, size)
                return self.ref.at[pl.ds(start, size), :]
            size = self.ref.shape[0] if size is None else size
            return self.ref.at[pl.ds(k * size, size), columns(index)]

        def start(self):
            for copy in self.over:
                copy.start()
            self.direct.start()

        def middle(self):
            for over, forward in zip(self.over, self.forward):
                over.wait_recv()
                forward.start()

        def finish(self):
            self.direct.wait_recv()
            for forward in self.forward:
                forward.wait_recv()
            sent.extend([self.direct] + self.over + self.forward)

    class Exchange:
        def __init__(self, src, dst, size):
            self.src, self.dst, self.size = src, dst, size
            self.sem = new_sem(n_grid)

        def block(self, ref, index):
            return ref.at[pl.ds(pl.multiple_of(index * self.size, self.size), self.size), :]

        def copy(self, step):
            to = (z + step) % n_grid
            return send(
                self.block(self.src, to), self.block(self.dst, z), self.sem + step, {"grid": to}
            )

        def start(self):
            repeat(n_grid - 1, lambda i: self.copy(i + 1).start())
            self.block(self.dst, z)[...] = self.block(self.src, z)[...]

        def finish(self):
            repeat(n_grid - 1, lambda i: self.copy(i + 1).wait_recv())

        def end(self):
            repeat(n_grid - 1, lambda i: self.copy(i + 1).wait_send())

    barrier = pltpu.get_barrier_semaphore()
    for partner in (side, cross):
        pl.semaphore_signal(barrier, inc=1, device_id={"feat": partner}, device_id_type=MESH)
    repeat(
        n_grid - 1,
        lambda i: pl.semaphore_signal(
            barrier, inc=1, device_id={"grid": (z + i + 1) % n_grid}, device_id_type=MESH
        ),
    )

    state_all[:, columns(f)] = mesh_state[...]
    gain_all[:, columns(f)] = jnp.concatenate(
        [enc_gain[...], proc_gain[...], jnp.zeros((7 - layers, part), F32)], axis=0
    )
    out_w_all[0, columns(f), :] = enc_out_w[...]
    for layer in range(layers):
        out_w_all[1 + layer, columns(f), :] = proc_out_w[layer]
    dec_w_all[:, columns(f)] = jnp.zeros((dec_w_all.shape[0], part), BF)
    dec_w_all[:variables, columns(f)] = dec_out_w[...]

    block = 128
    state_gather = Gather(state_all, False, 2)
    gain_gather = Gather(gain_all, False, 1)
    weight_gathers = [Gather(out_w_all.at[i], True, 1) for i in range(1 + layers)]
    dec_weight_gather = Gather(dec_w_all, False, 1)
    sum_gathers = [Gather(sums_all.at[i], False, nodes // block) for i in range(1 + layers)]
    dec_gather = Gather(dec_all, False, 2)
    enc_slots = Exchange(enc_out_slots, enc_in_slots, cap)
    enc_index = Exchange(enc_out_index, enc_in_index, cap)
    dec_slots = Exchange(dec_out_slots, dec_in_slots, cap2)
    dec_index = Exchange(dec_out_index, dec_in_index, cap2)

    pl.semaphore_wait(barrier, 2 + n_grid - 1)
    state_gather.start()

    grid_proj = dot_t(grid_state[...], enc_grid_w[...]).astype(BF)
    for i in range(n_grid // 4):
        parts = range(4 * i, 4 * i + 4)
        where = pl.ds(i * 4 * cap, 4 * cap)
        rows = jnp.concatenate([as_column(enc_rows[0, b : b + 1, :]) for b in parts], axis=0)
        enc_out_slots[where, :] = dot(hits(rows, grid_rows, 0), grid_proj).astype(BF)
        target = jnp.concatenate([as_column(enc_targets[0, b : b + 1, :]) for b in parts], axis=0)
        enc_out_index[where, :] = jnp.broadcast_to(target, (4 * cap, 128))
    enc_slots.start()
    enc_index.start()
    gain_gather.start()
    weight_gathers[0].start()

    def dec_prepare(b):
        where = pl.ds(pl.multiple_of(b * cap2, cap2), cap2)
        target = as_column(dec_targets[0, pl.ds(b, 1), :])
        dec_out_index[where, :] = jnp.broadcast_to(target, (cap2, 128))
        dec_pick[where, :] = hits(as_column(dec_rows[0, pl.ds(b, 1), :]), nodes, 0)

    repeat(n_grid, dec_prepare)
    dec_index.start()
    state_gather.middle()

    def edge_tile(j):
        where = pl.ds(pl.multiple_of(j * EDGE_TILE, EDGE_TILE), EDGE_TILE)
        to_row = receivers[pl.ds(j, 1), :]
        sender, receiver = as_column(senders[pl.ds(j, 1), :]), as_column(to_row)
        gather_sel[where, :nodes] = hits(sender, nodes, HALO)
        gather_sel[where, nodes : 2 * nodes] = hits(receiver, nodes, 0)
        lane = lax.broadcasted_iota(jnp.int32, (EDGE_TILE, 2 * HALO), 1)
        ends = jnp.where(lane < HALO, lane, lane + nodes).astype(F32)
        gather_sel[where, 2 * nodes :] = jnp.where(
            jnp.broadcast_to(sender, ends.shape) == ends, 1.0, 0.0
        ).astype(BF)
        row = lax.broadcasted_iota(jnp.int32, (nodes, EDGE_TILE), 0)
        scatter_sel[:, where] = jnp.where(
            jnp.broadcast_to(to_row, row.shape) == row, 1.0, 0.0
        ).astype(BF)

    def edge_tiles(first, last):
        lax.fori_loop(first, last, lambda j, c: (edge_tile(j), c)[1], 0)

    tiles = edges // EDGE_TILE
    edge_tiles(0, tiles // 2)

    state_gather.finish()
    mesh_proj = dot(state_all[...], enc_mesh_w[...]).astype(BF)
    enc_slots.finish()
    enc_index.finish()

    total = jnp.zeros((nodes, part), F32)
    chunk = 4 * cap
    for i in range(n_grid // 4):
        where = pl.ds(i * chunk, chunk)
        select = hits(enc_in_index[where, :], nodes, 0)
        before = enc_in_slots[where, :].astype(F32) + dot(select, mesh_proj) + enc_bias[...]
        total += dot_t(select, silu(before).astype(BF))
    sums_all[0, :, columns(f)] = total.astype(BF)
    sum_gathers[0].start()
    gain_gather.middle()
    weight_gathers[0].middle()
    edge_tiles(tiles // 2, tiles)

    def update(step):
        gather = sum_gathers[step]
        gather.middle()
        if step == 0:
            gain_gather.finish()
        weight_gathers[step].finish()
        gather.direct.wait_recv()
        for i in range(nodes // block):
            rows = slice(i * block, (i + 1) * block)
            gather.forward[i].wait_recv()
            u = dot(sums_all[step, rows, :], out_w_all[step])
            centre = jnp.mean(u, axis=1, keepdims=True)
            spread = jnp.mean(u * u, axis=1, keepdims=True) - centre * centre
            held = state_all[rows, :].astype(F32) if step == 0 else latent[rows, :]
            held += gain_all[step : step + 1, :] * ((u - centre) * lax.rsqrt(spread + 1e-05))
            latent[rows, :] = held
            latent_bf[rows, :] = held.astype(BF)
        sent.extend([gather.direct] + gather.over + gather.forward)

    update(0)
    right, left = (z + 1) % n_grid, (z + n_grid - 1) % n_grid
    for layer in range(layers):
        table[layer, :nodes, :] = dot(latent_bf[...], proc_send_w[layer]).astype(BF)
        up = send(
            table.at[layer, pl.ds(nodes - HALO, HALO), :],
            halo.at[layer, pl.ds(0, HALO), :],
            new_sem(),
            {"grid": right},
        )
        down = send(
            table.at[layer, pl.ds(0, HALO), :],
            halo.at[layer, pl.ds(HALO, HALO), :],
            new_sem(),
            {"grid": left},
        )
        up.start()
        down.start()
        weight_gathers[1 + layer].start()
        if layer == layers - 1:
            dec_weight_gather.start()
        table[layer, nodes:, :] = dot(latent_bf[...], proc_recv_w[layer]).astype(BF)
        for i in range(edges // EDGE_BLOCK):
            rows = slice(i * EDGE_BLOCK, (i + 1) * EDGE_BLOCK)
            pre[rows, :] = dot(gather_sel[rows, : 2 * nodes], table[layer])
        up.wait_recv()
        down.wait_recv()
        total = jnp.zeros((nodes, part), F32)
        for i in range(edges // EDGE_BLOCK):
            rows = slice(i * EDGE_BLOCK, (i + 1) * EDGE_BLOCK)
            before = pre[rows, :] + dot(gather_sel[rows, 2 * nodes :], halo[layer])
            hidden = silu(before + proc_bias[layer : layer + 1, :]).astype(BF)
            total += dot(scatter_sel[:, rows], hidden)
        sums_all[1 + layer, :, columns(f)] = total.astype(BF)
        sum_gathers[1 + layer].start()
        weight_gathers[1 + layer].middle()
        if layer == layers - 1:
            dec_weight_gather.middle()
        sent.extend([up, down])
        if layer == 0:
            dec_index.finish()
            query = dot_t(grid_state[...], dec_grid_w[...]).astype(BF)
            quarter = grid_rows // n_feat
            for i in range(n_grid // 4):
                where = pl.ds(i * 4 * cap2, 4 * cap2)
                targets = dec_in_index[where, :]
                dec_query[where, :] = dot(hits(targets, grid_rows, 0), query) + dec_bias[...]
                dec_spread[where, :] = hits(targets, quarter, f * quarter)
        update(1 + layer)

    mesh_out = dot(latent_bf[...], dec_mesh_w[...]).astype(BF)
    for i in range(n_grid // 4):
        where = pl.ds(i * 4 * cap2, 4 * cap2)
        dec_out_slots[where, :] = dot(dec_pick[where, :], mesh_out).astype(BF)
    dec_slots.start()
    dec_slots.finish()
    for i in range(n_grid // 4):
        where = pl.ds(i * 4 * cap2, 4 * cap2)
        before = dec_in_slots[where, :].astype(F32) + dec_query[where, :]
        dec_all[where, columns(f)] = silu(before).astype(BF)
    dec_gather.start()
    dec_weight_gather.finish()
    dec_gather.middle()
    dec_gather.finish()
    quarter = grid_rows // n_feat
    total = jnp.zeros((quarter, part * n_feat), F32)
    for i in range(n_grid // 4):
        where = pl.ds(i * 4 * cap2, 4 * cap2)
        total += dot_t(dec_spread[where, :], dec_all[where, :])
    own = grid_state[:, pl.ds(pl.multiple_of(f * quarter, quarter), quarter)]
    added = dot_n(dec_w_all[...], total.astype(BF))
    out[...] = own.astype(F32) + added[:variables, :]

    for copy in sent:
        copy.wait_send()
    for exchange in (enc_slots, enc_index, dec_slots, dec_index):
        exchange.end()


def local(
    grid_state,
    mesh_state,
    enc_rows,
    enc_targets,
    mesh_senders,
    mesh_receivers,
    dec_rows,
    dec_targets,
    enc_grid_w,
    enc_mesh_w,
    enc_bias,
    enc_out_w,
    enc_gain,
    proc_send_w,
    proc_recv_w,
    proc_bias,
    proc_out_w,
    proc_gain,
    dec_mesh_w,
    dec_grid_w,
    dec_bias,
    dec_out_w,
):
    n_grid, n_feat = lax.axis_size("grid"), lax.axis_size("feat")
    layers = proc_send_w.shape[0]
    nodes, part = mesh_state.shape
    width = part * n_feat
    grid_rows, variables = grid_state.shape
    enc_total = n_grid * enc_rows.shape[2]
    dec_total = n_grid * dec_rows.shape[2]
    edges = mesh_senders.shape[0]
    quarter = grid_rows // n_feat
    sems = 9 * 12 + 2 * layers + 4 * n_grid
    args = (
        grid_state.T,
        mesh_state,
        enc_rows,
        enc_targets,
        mesh_senders.reshape(-1, EDGE_TILE),
        mesh_receivers.reshape(-1, EDGE_TILE),
        dec_rows,
        dec_targets,
        enc_grid_w,
        enc_mesh_w,
        enc_bias.reshape(1, -1),
        enc_out_w,
        enc_gain.reshape(1, -1),
        proc_send_w,
        proc_recv_w,
        proc_bias,
        proc_out_w,
        proc_gain,
        dec_mesh_w,
        dec_grid_w,
        dec_bias.reshape(1, -1),
        dec_out_w.T,
    )
    return pl.pallas_call(
        functools.partial(kernel, n_grid, n_feat),
        out_shape=jax.ShapeDtypeStruct((variables, quarter), F32),
        in_specs=[pl.BlockSpec(memory_space=pltpu.VMEM)] * len(args),
        out_specs=pl.BlockSpec(memory_space=pltpu.VMEM),
        scratch_shapes=[
            pltpu.VMEM((nodes, width), BF),
            pltpu.VMEM((8, width), F32),
            pltpu.VMEM((1 + layers, width, width), BF),
            pltpu.VMEM((-(-variables // 16) * 16, width), BF),
            pltpu.VMEM((1 + layers, nodes, width), BF),
            pltpu.VMEM((dec_total, width), BF),
            pltpu.VMEM((enc_total, part), BF),
            pltpu.VMEM((enc_total, 128), F32),
            pltpu.VMEM((dec_total, part), BF),
            pltpu.VMEM((dec_total, 128), F32),
            pltpu.VMEM((enc_total, part), BF),
            pltpu.VMEM((enc_total, 128), F32),
            pltpu.VMEM((dec_total, part), BF),
            pltpu.VMEM((dec_total, 128), F32),
            pltpu.VMEM((dec_total, nodes), BF),
            pltpu.VMEM((dec_total, part), F32),
            pltpu.VMEM((dec_total, quarter), BF),
            pltpu.VMEM((edges, 2 * nodes + 2 * HALO), BF),
            pltpu.VMEM((nodes, edges), BF),
            pltpu.VMEM((edges, part), F32),
            pltpu.VMEM((layers, 2 * nodes, part), BF),
            pltpu.VMEM((layers, 2 * HALO, part), BF),
            pltpu.VMEM((nodes, width), F32),
            pltpu.VMEM((nodes, width), BF),
            pltpu.SemaphoreType.DMA((sems,)),
            pltpu.SemaphoreType.DMA((sems,)),
        ],
        compiler_params=pltpu.CompilerParams(
            collective_id=0, has_side_effects=True, vmem_limit_bytes=56 * 1024 * 1024
        ),
    )(*args).T


def solution(mesh):
    in_specs = (
        P(("groups", "grid"), None),
        P("grid", "feat"),
        P("grid", None, None),
        P("grid", None, None),
        P("grid"),
        P("grid"),
        P("grid", None, None),
        P("grid", None, None),
        P(None, "feat"),
        P(None, "feat"),
        P("feat"),
        P("feat", None),
        P("feat"),
        P(None, None, "feat"),
        P(None, None, "feat"),
        P(None, "feat"),
        P(None, "feat", None),
        P(None, "feat"),
        P(None, "feat"),
        P(None, "feat"),
        P("feat"),
        P("feat", None),
    )
    out_specs = P(("groups", "grid", "feat"), None)
    return jax.shard_map(local, mesh=mesh, in_specs=in_specs, out_specs=out_specs, check_vma=False)
```
